32 devices in a mesh: firm: 8 (over y, x, core), day: 4 (over z).
Axes of the slice: x: 2, y: 2, z: 4, core: 2. Of those that a mesh axis runs over, the one named last changes fastest.
Arguments:
- panel: float32 [65, 32, 4096], P(None, 'day', 'firm'), may hold values from -60 to 60, as said below
- presence: int32 [32, 4096], P(None, 'firm'), may hold values from 0 to 1, as said below
- firm_count: int32 [4096], P('firm'), may hold values from 1 to 32, as said below
- day_count: int32 [32], replicated, may hold values from 128 to 4096, as said below
Outputs:
- coefficients: float32 [64], replicated
- residual_panel: float32 [32, 4096], P('day', 'firm')
The draws below stay inside these ranges and needn't reach their ends.
Inputs may be any that keep to these rules, and one draw needn't show every extreme that they name: presence is 0 or 1; every firm has at least one entry and every day at least 128 entries; some firm is present on every day and some day holds every firm; presence rates differ strongly across firms and days. firm_count is the number of ones of presence in that firm's column. day_count is the number of ones of presence in that day's row. `panel`: values at absent entries are arbitrary and are not used.
All inputs are finite; a program needn't handle non-finite values.
Results may differ from the reference program's by a relative error of at most 0.00025.
Values sent between devices are 32-bit elements; how exact they have to be, the bound alone decides.
A program may use at most 64 MiB of HBM per device.

```python
import jax
import jax.numpy as jnp
from jax import lax

K = 64
COLS = 65
SWEEPS = 3
FIRMS = 4096
DAYS = 32


def presence_table(key):
    base = jax.random.fold_in(key, 31)
    key_firm, key_day, key_draw = jax.random.split(base, 3)
    firm_rate = jax.random.randint(key_firm, (FIRMS,), 150, 951)
    day_rate = jax.random.randint(key_day, (DAYS,), 400, 1001)
    limit = day_rate[:, None] * firm_rate[None, :] // 1000
    integer_draw = jax.random.randint(key_draw, (DAYS, FIRMS), 0, 1000)
    day_index = lax.broadcasted_iota(jnp.int32, (DAYS, FIRMS), 0)
    firm_index = lax.broadcasted_iota(jnp.int32, (DAYS, FIRMS), 1)
    forced = (day_index == firm_index % DAYS) | (day_index == 0) | (firm_index == 0)
    return jnp.where((integer_draw < limit) | forced, 1, 0).astype(jnp.int32)


def draw_presence(key, part):
    return presence_table(key)


def draw_firm_count(key, part):
    return jnp.sum(presence_table(key), axis=0).astype(jnp.int32)


def draw_day_count(key, part):
    return jnp.sum(presence_table(key), axis=1).astype(jnp.int32)


def draw_panel(key, part):
    base = jax.random.fold_in(key, 57)
    keys = jax.random.split(base, 4)
    noise = jax.random.normal(keys[0], (COLS, DAYS, FIRMS), jnp.float32)
    firm_effect = jax.random.normal(keys[1], (COLS, 1, FIRMS), jnp.float32)
    day_effect = 0.7 * jax.random.normal(keys[2], (COLS, DAYS, 1), jnp.float32)
    regress = jnp.clip(noise + firm_effect + day_effect, -25.0, 25.0)
    slopes = 1.5 * jax.random.normal(keys[3], (K,), jnp.float32) / jnp.sqrt(K * 1.0)
    returns = jnp.tensordot(slopes, regress[:K], axes=1) + regress[K]
    returns = jnp.clip(returns, -55.0, 55.0)
    return jnp.concatenate([regress[:K], returns[None]], axis=0).astype(jnp.float32)


def setup_inputs(seed: int = 0) -> dict:
    seeds = jax.random.split(jax.random.key(seed), 5)
    panel = draw_panel(jax.random.fold_in(seeds[4], 71), 0)
    presence = draw_presence(jax.random.fold_in(seeds[4], 71), 0)
    firm_count = draw_firm_count(jax.random.fold_in(seeds[4], 71), 0)
    day_count = draw_day_count(jax.random.fold_in(seeds[4], 71), 0)
    return {"panel": panel, "presence": presence, "firm_count": firm_count, "day_count": day_count}


def sweep_column(column, mask_f, firm_n, day_n):
    current = column * mask_f
    for sweep in range(SWEEPS):
        firm_mean = jnp.sum(current, axis=0) / firm_n
        demeaned = mask_f * (current - firm_mean[None, :])
        day_mean = jnp.sum(demeaned, axis=1) / day_n
        current = mask_f * (demeaned - day_mean[:, None])
    return current

def reference(panel, presence, firm_count, day_count):
    mask_f = presence.astype(jnp.float32)
    firm_n = firm_count.astype(jnp.float32)
    day_n = day_count.astype(jnp.float32)
    demeaned = lax.map(lambda column: sweep_column(column, mask_f, firm_n, day_n), panel)
    flat = demeaned.reshape(demeaned.shape[0], -1)
    gram = jnp.dot(flat, flat.T, precision=lax.Precision.HIGHEST)
    matrix = gram[:K, :K]
    target = gram[:K, K:]
    factor = jnp.linalg.cholesky(matrix)
    middle = lax.linalg.triangular_solve(factor, target, left_side=True, lower=True)
    coefficients = lax.linalg.triangular_solve(factor, middle, left_side=True, lower=True, transpose_a=True)[:, 0]
    fitted = jnp.tensordot(coefficients, demeaned[:K], axes=1, precision=lax.Precision.HIGHEST)
    residual_panel = mask_f * (demeaned[K] - fitted)
    return (coefficients, residual_panel)
```

```python
import functools

import jax
import jax.numpy as jnp
from jax import lax
from jax.experimental import pallas as pl
from jax.experimental.pallas import tpu as pltpu
from jax.sharding import PartitionSpec as P

SWEEPS = 3
HIGHEST = lax.Precision.HIGHEST
MESH = pl.DeviceIdType.MESH


def up(n, m):
    return -(-n // m) * m


def nt(a, b):
    return lax.dot_general(
        a, b, (((1,), (1,)), ((), ())), precision=HIGHEST, preferred_element_type=jnp.float32
    )


def nn(a, b):
    return jnp.dot(a, b, precision=HIGHEST, preferred_element_type=jnp.float32)


def kernel(
    nf, nd, panel, presence, coef_ref, resid_ref,
    big, means, means_all, masks, alphas, alphas_in, part, part_in, mid, mid_in, full, vfull,
    s_a, r_a, s_m, r_m, s_1, r_1, s_2, r_2, s_3, r_3,
):
    cols, day_dev, firm_dev = panel.shape
    regs = cols - 1
    days = presence.shape[0]
    chunk = firm_dev // nd
    crow = up(cols, 8)
    width = full.shape[2]
    f = lax.axis_index("firm")
    d = lax.axis_index("day")

    def firm_peer(o):
        return lax.rem(f + o, nf)

    def day_peer(o):
        return lax.rem(d + o, nd)

    barrier = pltpu.get_barrier_semaphore()
    for o in range(1, nf):
        pl.semaphore_signal(barrier, inc=1, device_id=(firm_peer(o), d), device_id_type=MESH)
    for o in range(1, nd):
        pl.semaphore_signal(barrier, inc=1, device_id=(f, day_peer(o)), device_id_type=MESH)

    def send_day(o, src, dst, ssem, rsem):
        return pltpu.make_async_remote_copy(
            src_ref=src, dst_ref=dst, send_sem=ssem.at[o], recv_sem=rsem,
            device_id=(f, day_peer(o)), device_id_type=MESH)

    def send_firm(o, src, dst, ssem, rsem):
        return pltpu.make_async_remote_copy(
            src_ref=src, dst_ref=dst, send_sem=ssem.at[o], recv_sem=rsem,
            device_id=(firm_peer(o), d), device_id_type=MESH)

    mask = presence[...].astype(jnp.float32)
    for j in range(nd):
        masks[j] = mask[:, j * chunk:(j + 1) * chunk]
    here = presence[pl.ds(pl.multiple_of(d * day_dev, 8), day_dev), :].astype(jnp.float32)
    here_n = jnp.maximum(jnp.sum(here, axis=0, keepdims=True), 1.0)
    total = jnp.zeros((cols, firm_dev), jnp.float32)
    for t in range(day_dev):
        total = total + panel[:, t, :] * here[t:t + 1, :]
    alpha = total / here_n
    alphas[:, cols:, :] = jnp.zeros((nd, crow - cols, chunk), jnp.float32)
    for j in range(nd):
        alphas[j, :cols, :] = alpha[:, j * chunk:(j + 1) * chunk]
    pl.semaphore_wait(barrier, nf + nd - 2)
    sends = []
    for o in range(1, nd):
        c = send_day(o, alphas.at[day_peer(o)], alphas_in.at[d], s_a, r_a.at[d])
        c.start()
        sends.append(c)
    alphas_in[d] = alphas[d]

    big[cols:crow, :] = jnp.zeros((crow - cols, day_dev * firm_dev), jnp.float32)
    row_id = lax.broadcasted_iota(jnp.int32, (days, firm_dev), 0)
    for t in range(day_dev):
        lanes = slice(t * firm_dev, (t + 1) * firm_dev)
        big[:cols, lanes] = here[t:t + 1, :] * (panel[:, t, :] - alpha)
        big[crow:crow + days, lanes] = (row_id == d * day_dev + t).astype(jnp.float32)
    gram = nt(big[:crow, :], big[...])

    for o in range(1, nd):
        src = day_peer(o)
        send_day(o, alphas.at[src], alphas_in.at[src], s_a, r_a.at[src]).wait_recv()
    own = masks[d]
    counts = [
        jnp.sum(own[j * day_dev:(j + 1) * day_dev, :], axis=0, keepdims=True) for j in range(nd)
    ]
    n = functools.reduce(jnp.add, counts)
    blocks = [alphas_in[j] for j in range(nd)]
    mean = functools.reduce(jnp.add, [b * w for b, w in zip(blocks, counts)]) / n
    means_all[d] = mean
    for o in range(1, nd):
        c = send_day(o, means_all.at[d], means_all.at[d], s_m, r_m.at[d])
        c.start()
        sends.append(c)
    day_id = lax.broadcasted_iota(jnp.int32, (days, chunk), 0)
    for j in range(nd):
        delta = blocks[j] - mean
        lo = j * day_dev
        dummy = jnp.where((day_id >= lo) & (day_id < lo + day_dev), own, 0.0)
        gram = gram + nt(delta, jnp.concatenate([delta * counts[j], dummy], axis=0))
    share = nt(own, jnp.concatenate([jnp.zeros((crow, chunk), jnp.float32), own / n], axis=0))

    size = crow + days
    piece = part.shape[1]
    table = jnp.concatenate([gram, share], axis=0)
    if nf * piece > size:
        table = jnp.concatenate([table, jnp.zeros((nf * piece - size, size), jnp.float32)], axis=0)
    if width > size:
        table = jnp.concatenate([table, jnp.zeros((nf * piece, width - size), jnp.float32)], axis=1)
    part[...] = table.reshape(nf, piece, width)
    for o in range(1, nf):
        c = send_firm(o, part.at[firm_peer(o)], part_in.at[f], s_1, r_1.at[f])
        c.start()
        sends.append(c)
    part_in[f] = part[f]
    for o in range(1, nf):
        src = firm_peer(o)
        send_firm(o, part.at[src], part_in.at[src], s_1, r_1.at[src]).wait_recv()
    mid[d] = functools.reduce(jnp.add, [part_in[j] for j in range(nf)])
    for o in range(1, nd):
        c = send_day(o, mid.at[d], mid.at[d], s_2, r_2.at[d])
        c.start()
        sends.append(c)
    for o in range(1, nd):
        src = day_peer(o)
        send_day(o, mid.at[src], mid.at[src], s_2, r_2.at[src]).wait_recv()
    full[f] = functools.reduce(jnp.add, [mid[j] for j in range(nd)])
    for o in range(1, nf):
        c = send_firm(o, full.at[f], full.at[f], s_3, r_3.at[f])
        c.start()
        sends.append(c)
    for o in range(1, nf):
        src = firm_peer(o)
        send_firm(o, full.at[src], full.at[src], s_3, r_3.at[src]).wait_recv()

    table = full[...].reshape(nf * piece, width)
    gram = table[:crow, :crow]
    csum = table[:crow, crow:size]
    share = table[crow:size, crow:size]
    day_n = jnp.floor(jnp.sum(share, axis=0, keepdims=True) + 0.5)
    before = csum / day_n
    after = before
    for _ in range(SWEEPS - 1):
        before, after = after, (csum + nn(after, share)) / day_n
    step = after - before
    excess = step * day_n
    gram = gram - nt(csum, before) - nt(before, excess) - nt(excess, step)

    for o in range(1, nd):
        src = day_peer(o)
        send_day(o, means_all.at[src], means_all.at[src], s_m, r_m.at[src]).wait_recv()
    for j in range(nd):
        means[:, j * chunk:(j + 1) * chunk] = means_all[j]
    n_all = jnp.sum(mask, axis=0, keepdims=True)
    firm_eff = means[...] - nn(before, mask) / n_all
    after_t = after.T
    full_days = after_t[:days, :]

    aug = gram[:regs, :]
    rid = lax.broadcasted_iota(jnp.int32, aug.shape, 0)
    lid = lax.broadcasted_iota(jnp.int32, aug.shape, 1)
    for k in range(regs):
        row = aug[k:k + 1, :] / aug[k:k + 1, k:k + 1]
        col = jnp.where(rid[:, :1] == k, 0.0, aug[:, k:k + 1])
        aug = aug - col * row
    diag = jnp.sum(jnp.where(rid == lid, aug, 0.0), axis=1, keepdims=True)
    coef = aug[:, regs:regs + 1] / diag
    sq = (regs, regs)
    eye = lax.broadcasted_iota(jnp.int32, sq, 0) == lax.broadcasted_iota(jnp.int32, sq, 1)
    coef_ref[...] = jnp.sum(jnp.where(eye, coef, 0.0), axis=0, keepdims=True)

    vfull[...] = jnp.zeros(vfull.shape, jnp.float32)
    vfull[:regs, :] = jnp.broadcast_to(-coef, (regs, vfull.shape[1]))
    vfull[regs:cols, :] = jnp.ones((1, vfull.shape[1]), jnp.float32)
    v = vfull[:, :1]
    firm_part = jnp.sum(firm_eff * v, axis=0, keepdims=True)
    day_part = jnp.sum(after * v, axis=0, keepdims=True)
    day_sel = (lax.broadcasted_iota(jnp.int32, (day_dev, days), 1)
               == lax.broadcasted_iota(jnp.int32, (day_dev, days), 0) + d * day_dev)
    day_here = jnp.sum(jnp.where(day_sel, day_part, 0.0), axis=1, keepdims=True)
    acc = jnp.zeros((day_dev, firm_dev), jnp.float32)
    for c in range(cols):
        acc = acc + panel[c] * vfull[c:c + 1, :1]
    resid_ref[...] = here * (acc - firm_part - day_here)

    for c in sends:
        c.wait_send()


def on_device(nf, nd, panel, presence, firm_count, day_count):
    cols, day_dev, firm_dev = panel.shape
    days = presence.shape[0]
    chunk = firm_dev // nd
    crow = up(cols, 8)
    size = crow + days
    piece = up(-(-size // nf), 8)
    width = up(size, 128)
    vm = pl.BlockSpec(memory_space=pltpu.VMEM)
    f32 = jnp.float32
    dma = pltpu.SemaphoreType.DMA
    coef, resid = pl.pallas_call(
        functools.partial(kernel, nf, nd),
        out_shape=(jax.ShapeDtypeStruct((1, cols - 1), f32),
                   jax.ShapeDtypeStruct((day_dev, firm_dev), f32)),
        in_specs=[vm, vm],
        out_specs=(vm, vm),
        scratch_shapes=[
            pltpu.VMEM((size, day_dev * firm_dev), f32),
            pltpu.VMEM((crow, firm_dev), f32),
            pltpu.VMEM((nd, crow, chunk), f32),
            pltpu.VMEM((nd, days, chunk), f32),
            pltpu.VMEM((nd, crow, chunk), f32),
            pltpu.VMEM((nd, crow, chunk), f32),
            pltpu.VMEM((nf, piece, width), f32),
            pltpu.VMEM((nf, piece, width), f32),
            pltpu.VMEM((nd, piece, width), f32),
            pltpu.VMEM((8, 128), f32),
            pltpu.VMEM((nf, piece, width), f32),
            pltpu.VMEM((crow, 128), f32),
            dma((nd,)), dma((nd,)), dma((nd,)), dma((nd,)),
            dma((nf,)), dma((nf,)), dma((nd,)), dma((nd,)), dma((nf,)), dma((nf,)),
        ],
        compiler_params=pltpu.CompilerParams(
            collective_id=0, has_side_effects=True, vmem_limit_bytes=40 * 2**20
        ),
    )(panel, presence)
    return coef.reshape(cols - 1), resid


def solution(mesh):
    placed = (P(None, "day", "firm"), P(None, "firm"), P("firm"), P())
    body = functools.partial(on_device, mesh.shape["firm"], mesh.shape["day"])
    return jax.shard_map(
        body, mesh=mesh, in_specs=placed, out_specs=(P(), P("day", "firm")), check_vma=False
    )
```

```python
import functools

import jax
import jax.numpy as jnp
from jax import lax
from jax.experimental import pallas as pl
from jax.experimental.pallas import tpu as pltpu
from jax.sharding import PartitionSpec as P

SWEEPS = 3
HIGHEST = lax.Precision.HIGHEST
MESH = pl.DeviceIdType.MESH


def up(n, m):
    return -(-n // m) * m


def nt(a, b):
    return lax.dot_general(
        a, b, (((1,), (1,)), ((), ())), precision=HIGHEST, preferred_element_type=jnp.float32
    )


def nn(a, b):
    return jnp.dot(a, b, precision=HIGHEST, preferred_element_type=jnp.float32)


def split(x):
    hi = x.astype(jnp.bfloat16)
    return hi, (x - hi.astype(jnp.float32)).astype(jnp.bfloat16)


def nt16(a, b):
    return lax.dot_general(a, b, (((1,), (1,)), ((), ())), preferred_element_type=jnp.float32)


def inverse2(p):
    (a, b), (c, e) = p
    r = 1.0 / (a * e - b * c)
    return [[e * r, -b * r], [-c * r, a * r]]


def times(p, rows):
    return [p[0][0] * rows[0] + p[0][1] * rows[1], p[1][0] * rows[0] + p[1][1] * rows[1]]


def solve4(p, rows):
    top = inverse2([p[0][:2], p[1][:2]])
    right = [[p[0][2], p[0][3]], [p[1][2], p[1][3]]]
    low = [p[2][:2], p[3][:2]]
    cols = [times(top, [right[0][j], right[1][j]]) for j in range(2)]
    schur = [[None, None], [None, None]]
    for j in range(2):
        down = times(low, cols[j])
        for i in range(2):
            schur[i][j] = p[2 + i][2 + j] - down[i]
    bottom = inverse2(schur)
    up_rows = times(top, rows[:2])
    down = times(low, up_rows)
    under = times(bottom, [rows[2] - down[0], rows[3] - down[1]])
    return [
        up_rows[0] - cols[0][0] * under[0] - cols[1][0] * under[1],
        up_rows[1] - cols[0][1] * under[0] - cols[1][1] * under[1],
    ] + under


def eliminate(mat, regs):
    tiles = [mat[8 * i:8 * i + 8, :] for i in range(regs // 8)]
    shape = tiles[0].shape
    sub = lax.broadcasted_iota(jnp.int32, shape, 0)
    for k in range(0, regs, 4):
        at, lo = k // 8, k % 8
        col = [[jnp.broadcast_to(t[:, k + j:k + j + 1], shape) for t in tiles] for j in range(4)]
        p = [[col[j][at][lo + i:lo + i + 1, :] for j in range(4)] for i in range(4)]
        rows = solve4(p, [tiles[at][lo + i:lo + i + 1, :] for i in range(4)])
        out = []
        for i, t in enumerate(tiles):
            t = t - (col[0][i] * rows[0] + col[1][i] * rows[1]) - (col[2][i] * rows[2] + col[3][i] * rows[3])
            if i == at:
                for j in range(4):
                    t = jnp.where(sub == lo + j, rows[j], t)
            out.append(t)
        tiles = out
    return tiles


def kernel(
    nf, nd, panel_hbm, presence_hbm, coef_ref, resid_ref,
    panel, presence, big, left, right, means, means_all, masks, alphas, alphas_in,
    part, part_in, mid, full, vfull,
    s_in, s_a, r_a, s_m, r_m, s_1, r_1, s_2, r_2, s_3, r_3,
):
    cols, day_dev, firm_dev = panel_hbm.shape
    regs = cols - 1
    days = presence.shape[0]
    chunk = firm_dev // nd
    crow = up(cols, 8)
    xrow = panel.shape[0]
    half = right.shape[0] // 2
    piece, width = part.shape[1:]
    f = lax.axis_index("firm")
    d = lax.axis_index("day")
    f32 = jnp.float32

    def firm_peer(o):
        return lax.rem(f + o, nf)

    def day_peer(o):
        return lax.rem(d + o, nd)

    load_mask = pltpu.make_async_copy(presence_hbm, presence, s_in.at[0])
    load_mask.start()
    load_panel = pltpu.make_async_copy(panel_hbm, panel.at[pl.ds(0, cols)], s_in.at[1])
    load_panel.start()
    barrier = pltpu.get_barrier_semaphore()
    for o in range(1, nf):
        pl.semaphore_signal(barrier, inc=1, device_id=(firm_peer(o), d), device_id_type=MESH)
    for o in range(1, nd):
        pl.semaphore_signal(barrier, inc=1, device_id=(f, day_peer(o)), device_id_type=MESH)

    def send_day(o, src, dst, ssem, rsem):
        return pltpu.make_async_remote_copy(
            src_ref=src, dst_ref=dst, send_sem=ssem.at[o], recv_sem=rsem,
            device_id=(f, day_peer(o)), device_id_type=MESH)

    def send_firm(o, src, dst, ssem, rsem):
        return pltpu.make_async_remote_copy(
            src_ref=src, dst_ref=dst, send_sem=ssem.at[o], recv_sem=rsem,
            device_id=(firm_peer(o), d), device_id_type=MESH)

    panel[cols:, :, :] = jnp.zeros((xrow - cols, day_dev, firm_dev), f32)
    row_id = lax.broadcasted_iota(jnp.int32, (half - xrow, firm_dev), 0)
    for t in range(day_dev):
        lanes = slice(t * firm_dev, (t + 1) * firm_dev)
        big[xrow:half, lanes] = (row_id == d * day_dev + t).astype(f32).astype(jnp.bfloat16)
    if half > xrow:
        big[half + xrow:, :] = jnp.zeros((half - xrow, day_dev * firm_dev), jnp.bfloat16)
    load_mask.wait()
    mask = presence[...].astype(f32)
    for j in range(nd):
        masks[j] = mask[:, j * chunk:(j + 1) * chunk]
    here = presence[pl.ds(pl.multiple_of(d * day_dev, 8), day_dev), :].astype(f32)
    here_n = jnp.maximum(jnp.sum(here, axis=0, keepdims=True), 1.0)
    own = masks[d]
    counts = [
        jnp.sum(own[j * day_dev:(j + 1) * day_dev, :], axis=0, keepdims=True) for j in range(nd)
    ]
    n = functools.reduce(jnp.add, counts)
    day_id = lax.broadcasted_iota(jnp.int32, (days, chunk), 0)
    share = split(own / n)
    fill = jnp.zeros((xrow - crow, chunk), f32)
    tail = [jnp.zeros((half - xrow - days, chunk), f32)] if half > xrow + days else []

    load_panel.wait()
    total = panel[:crow, 0, :] * here[0:1, :]
    for t in range(1, day_dev):
        total = total + panel[:crow, t, :] * here[t:t + 1, :]
    alpha = total / here_n
    for j in range(nd):
        alphas[j] = alpha[:, j * chunk:(j + 1) * chunk]
    pl.semaphore_wait(barrier, nf + nd - 2)
    sends = []
    for o in range(1, nd):
        c = send_day(o, alphas.at[day_peer(o)], alphas_in.at[d], s_a, r_a.at[d])
        c.start()
        sends.append(c)
    alphas_in[d] = alphas[d]

    base = jnp.concatenate([alpha, jnp.zeros((xrow - crow, firm_dev), f32)], axis=0)
    for t in range(day_dev):
        lanes = slice(t * firm_dev, (t + 1) * firm_dev)
        hi, lo = split(here[t:t + 1, :] * (panel[:, t, :] - base))
        big[:xrow, lanes] = hi
        big[half:half + xrow, lanes] = lo
    inner = nt16(jnp.concatenate([big[:xrow, :], big[half:half + xrow, :]], axis=0), big[...])

    for o in range(1, nd):
        src = day_peer(o)
        send_day(o, alphas.at[src], alphas_in.at[src], s_a, r_a.at[src]).wait_recv()
    blocks = [alphas_in[j] for j in range(nd)]
    mean = functools.reduce(jnp.add, [b * w for b, w in zip(blocks, counts)]) / n
    means_all[d] = mean
    for j in range(nd):
        lanes = slice(j * chunk, (j + 1) * chunk)
        delta = jnp.concatenate([blocks[j] - mean, fill], axis=0)
        first = j * day_dev
        dummy = jnp.where((day_id >= first) & (day_id < first + day_dev), own, 0.0)
        hi, lo = split(delta)
        left[:xrow, lanes] = hi
        left[xrow:2 * xrow, lanes] = lo
        left[2 * xrow:2 * xrow + days, lanes] = share[0]
        left[2 * xrow + days:, lanes] = share[1]
        hi, lo = split(jnp.concatenate([delta * counts[j], dummy] + tail, axis=0))
        right[:half, lanes] = hi
        right[half:, lanes] = lo
    outer = nt16(left[...], right[...])
    both = inner + outer[:2 * xrow, :]
    both = both[:, :half] + both[:, half:]
    table = jnp.concatenate(
        [both[:xrow, :] + both[xrow:, :],
         outer[2 * xrow:2 * xrow + days, :half] + outer[2 * xrow + days:, :half]], axis=0
    )

    if nf * piece > xrow + days:
        table = jnp.concatenate([table, jnp.zeros((nf * piece - xrow - days, width), f32)], axis=0)
    part[...] = table.reshape(nf, piece, width)
    for o in range(1, nf):
        c = send_firm(o, part.at[firm_peer(o)], part_in.at[f], s_1, r_1.at[f])
        c.start()
        sends.append(c)
    part_in[f] = part[f]
    for o in range(1, nf):
        src = firm_peer(o)
        send_firm(o, part.at[src], part_in.at[src], s_1, r_1.at[src]).wait_recv()
    mid[d] = functools.reduce(jnp.add, [part_in[j] for j in range(nf)])
    for o in range(1, nd):
        c = send_day(o, mid.at[d], mid.at[d], s_2, r_2.at[d])
        c.start()
        sends.append(c)
    for o in range(1, nd):
        c = send_day(o, means_all.at[d], means_all.at[d], s_m, r_m.at[d])
        c.start()
        sends.append(c)
    for o in range(1, nd):
        src = day_peer(o)
        send_day(o, mid.at[src], mid.at[src], s_2, r_2.at[src]).wait_recv()
    full[f] = functools.reduce(jnp.add, [mid[j] for j in range(nd)])
    for o in range(1, nf):
        c = send_firm(o, full.at[f], full.at[f], s_3, r_3.at[f])
        c.start()
        sends.append(c)
    for o in range(1, nf):
        src = firm_peer(o)
        send_firm(o, full.at[src], full.at[src], s_3, r_3.at[src]).wait_recv()

    table = full[...].reshape(nf * piece, width)
    csum = table[:xrow, xrow:xrow + days]
    cross = table[xrow:xrow + days, xrow:xrow + days]
    day_n = jnp.floor(jnp.sum(cross, axis=0, keepdims=True) + 0.5)
    before = csum / day_n
    after = before
    for _ in range(SWEEPS - 1):
        before, after = after, (csum + nn(after, cross)) / day_n
    step = after - before
    excess = step * day_n
    gram = table[:regs, :xrow] - (
        nt(csum[:regs], before) + nt(before[:regs], excess) + nt(excess[:regs], step)
    )

    tiles = eliminate(gram, regs)
    shape = (8, vfull.shape[1])
    sub = lax.broadcasted_iota(jnp.int32, shape, 0)
    lane = lax.broadcasted_iota(jnp.int32, shape, 1)
    picked = jnp.zeros(shape, f32)
    for i, t in enumerate(tiles):
        value = jnp.broadcast_to(t[:, regs:regs + 1], shape)
        vfull[8 * i:8 * i + 8, :] = -value
        picked = picked + jnp.where(lane == sub + 8 * i, value, 0.0)
    coef_ref[...] = jnp.sum(picked, axis=0, keepdims=True)[:, :regs]
    vfull[regs:, :] = jnp.where(
        lax.broadcasted_iota(jnp.int32, (xrow - regs, vfull.shape[1]), 0) == 0, 1.0, 0.0
    )

    acc = panel[0] * vfull[0:1, :1]
    for c in range(1, cols):
        acc = acc + panel[c] * vfull[c:c + 1, :1]
    v = vfull[:, :1]
    hi, lo = split(jnp.broadcast_to(jnp.sum(before * v, axis=0, keepdims=True), (8, days)))
    lead = jnp.concatenate([hi, lo], axis=0)
    spread = jnp.dot(lead, mask.astype(jnp.bfloat16), preferred_element_type=f32)
    spread = spread[0:1, :] + spread[8:9, :]
    day_part = jnp.sum(after * v, axis=0, keepdims=True)
    day_sel = (lax.broadcasted_iota(jnp.int32, (day_dev, days), 1)
               == lax.broadcasted_iota(jnp.int32, (day_dev, days), 0) + d * day_dev)
    day_here = jnp.sum(jnp.where(day_sel, day_part, 0.0), axis=1, keepdims=True)
    for o in range(1, nd):
        src = day_peer(o)
        send_day(o, means_all.at[src], means_all.at[src], s_m, r_m.at[src]).wait_recv()
    for j in range(nd):
        means[:, j * chunk:(j + 1) * chunk] = means_all[j]
    n_all = jnp.sum(mask, axis=0, keepdims=True)
    firm_part = jnp.sum(means[...] * vfull[:crow, :1], axis=0, keepdims=True) - spread / n_all
    resid_ref[...] = here * (acc - firm_part - day_here)

    for c in sends:
        c.wait_send()


def on_device(nf, nd, panel, presence, firm_count, day_count):
    cols, day_dev, firm_dev = panel.shape
    days = presence.shape[0]
    chunk = firm_dev // nd
    crow = up(cols, 8)
    xrow = up(cols, 16)
    half = up(xrow + days, 128)
    piece = up(-(-(xrow + days) // nf), 8)
    anywhere = pl.BlockSpec(memory_space=pl.ANY)
    vm = pl.BlockSpec(memory_space=pltpu.VMEM)
    f32 = jnp.float32
    b16 = jnp.bfloat16
    dma = pltpu.SemaphoreType.DMA
    coef, resid = pl.pallas_call(
        functools.partial(kernel, nf, nd),
        out_shape=(jax.ShapeDtypeStruct((1, cols - 1), f32),
                   jax.ShapeDtypeStruct((day_dev, firm_dev), f32)),
        in_specs=[anywhere, anywhere],
        out_specs=(vm, vm),
        scratch_shapes=[
            pltpu.VMEM((xrow, day_dev, firm_dev), f32),
            pltpu.VMEM((days, firm_dev), jnp.int32),
            pltpu.VMEM((2 * half, day_dev * firm_dev), b16),
            pltpu.VMEM((2 * (xrow + days), firm_dev), b16),
            pltpu.VMEM((2 * half, firm_dev), b16),
            pltpu.VMEM((crow, firm_dev), f32),
            pltpu.VMEM((nd, crow, chunk), f32),
            pltpu.VMEM((nd, days, chunk), f32),
            pltpu.VMEM((nd, crow, chunk), f32),
            pltpu.VMEM((nd, crow, chunk), f32),
            pltpu.VMEM((nf, piece, half), f32),
            pltpu.VMEM((nf, piece, half), f32),
            pltpu.VMEM((nd, piece, half), f32),
            pltpu.VMEM((nf, piece, half), f32),
            pltpu.VMEM((xrow, 128), f32),
            dma((2,)), dma((nd,)), dma((nd,)), dma((nd,)), dma((nd,)),
            dma((nf,)), dma((nf,)), dma((nd,)), dma((nd,)), dma((nf,)), dma((nf,)),
        ],
        compiler_params=pltpu.CompilerParams(collective_id=0, has_side_effects=True),
    )(panel, presence)
    return coef.reshape(cols - 1), resid


def solution(mesh):
    placed = (P(None, "day", "firm"), P(None, "firm"), P("firm"), P())
    body = functools.partial(on_device, mesh.shape["firm"], mesh.shape["day"])
    return jax.shard_map(
        body, mesh=mesh, in_specs=placed, out_specs=(P(), P("day", "firm")), check_vma=False
    )
```

```python
import functools

import jax
import jax.numpy as jnp
from jax import lax
from jax.experimental import pallas as pl
from jax.experimental.pallas import tpu as pltpu
from jax.sharding import PartitionSpec as P

SWEEPS = 3
HIGHEST = lax.Precision.HIGHEST
MESH = pl.DeviceIdType.MESH


def up(n, m):
    return -(-n // m) * m


def nt(a, b):
    return lax.dot_general(
        a, b, (((1,), (1,)), ((), ())), precision=HIGHEST, preferred_element_type=jnp.float32
    )


def nn(a, b):
    return jnp.dot(a, b, precision=HIGHEST, preferred_element_type=jnp.float32)


def split(x):
    hi = x.astype(jnp.bfloat16)
    return hi, (x - hi.astype(jnp.float32)).astype(jnp.bfloat16)


def nt16(a, b):
    return lax.dot_general(a, b, (((1,), (1,)), ((), ())), preferred_element_type=jnp.float32)


def inverse2(p):
    (a, b), (c, e) = p
    r = 1.0 / (a * e - b * c)
    return [[e * r, -b * r], [-c * r, a * r]]


def times(p, rows):
    return [p[0][0] * rows[0] + p[0][1] * rows[1], p[1][0] * rows[0] + p[1][1] * rows[1]]


def solve4(p, rows):
    top = inverse2([p[0][:2], p[1][:2]])
    right = [[p[0][2], p[0][3]], [p[1][2], p[1][3]]]
    low = [p[2][:2], p[3][:2]]
    cols = [times(top, [right[0][j], right[1][j]]) for j in range(2)]
    schur = [[None, None], [None, None]]
    for j in range(2):
        down = times(low, cols[j])
        for i in range(2):
            schur[i][j] = p[2 + i][2 + j] - down[i]
    bottom = inverse2(schur)
    up_rows = times(top, rows[:2])
    down = times(low, up_rows)
    under = times(bottom, [rows[2] - down[0], rows[3] - down[1]])
    return [
        up_rows[0] - cols[0][0] * under[0] - cols[1][0] * under[1],
        up_rows[1] - cols[0][1] * under[0] - cols[1][1] * under[1],
    ] + under


def eliminate(mat, regs):
    tiles = [mat[8 * i:8 * i + 8, :] for i in range(regs // 8)]
    shape = tiles[0].shape
    sub = lax.broadcasted_iota(jnp.int32, shape, 0)
    for k in range(0, regs, 4):
        at, lo = k // 8, k % 8
        col = [[jnp.broadcast_to(t[:, k + j:k + j + 1], shape) for t in tiles] for j in range(4)]
        p = [[col[j][at][lo + i:lo + i + 1, :] for j in range(4)] for i in range(4)]
        rows = solve4(p, [tiles[at][lo + i:lo + i + 1, :] for i in range(4)])
        out = []
        for i, t in enumerate(tiles):
            t = t - (col[0][i] * rows[0] + col[1][i] * rows[1]) - (col[2][i] * rows[2] + col[3][i] * rows[3])
            if i == at:
                for j in range(4):
                    t = jnp.where(sub == lo + j, rows[j], t)
            out.append(t)
        tiles = out
    return tiles


def kernel(
    nf, nd, panel_hbm, presence_hbm, coef_ref, resid_ref,
    panel, presence, big, left, right, means, means_all, masks, alphas, alphas_in,
    part, part_in, mid, full, vfull,
    s_in, s_a, r_a, s_m, r_m, s_1, r_1, s_2, r_2, s_3, r_3,
):
    day_dev, firm_dev = resid_ref.shape
    cols = panel_hbm.shape[0] // day_dev
    regs = cols - 1
    days = presence.shape[0]
    chunk = firm_dev // nd
    crow = up(cols, 8)
    xrow = panel.shape[1] // day_dev
    tiles128 = range(firm_dev // 128)
    half = right.shape[0] // 2
    piece, width = part.shape[1:]
    f = lax.axis_index("firm")
    d = lax.axis_index("day")
    f32 = jnp.float32

    def firm_peer(o):
        return lax.rem(f + o, nf)

    def day_peer(o):
        return lax.rem(d + o, nd)

    load_mask = pltpu.make_async_copy(presence_hbm, presence, s_in.at[0])
    load_mask.start()
    load_panel = [
        pltpu.make_async_copy(
            panel_hbm.at[:, pl.ds(q * 128, 128)], panel.at[q, pl.ds(0, cols * day_dev)], s_in.at[1 + q])
        for q in tiles128
    ]
    for c in load_panel:
        c.start()
    barrier = pltpu.get_barrier_semaphore()
    for o in range(1, nf):
        pl.semaphore_signal(barrier, inc=1, device_id=(firm_peer(o), d), device_id_type=MESH)
    for o in range(1, nd):
        pl.semaphore_signal(barrier, inc=1, device_id=(f, day_peer(o)), device_id_type=MESH)

    def send_day(o, src, dst, ssem, rsem):
        return pltpu.make_async_remote_copy(
            src_ref=src, dst_ref=dst, send_sem=ssem.at[o], recv_sem=rsem,
            device_id=(f, day_peer(o)), device_id_type=MESH)

    def send_firm(o, src, dst, ssem, rsem):
        return pltpu.make_async_remote_copy(
            src_ref=src, dst_ref=dst, send_sem=ssem.at[o], recv_sem=rsem,
            device_id=(firm_peer(o), d), device_id_type=MESH)

    panel[:, cols * day_dev:, :] = jnp.zeros((len(tiles128), (xrow - cols) * day_dev, 128), f32)

    def on_day(q, t, rows):
        return panel[q, pl.ds(t, rows, stride=day_dev), :]

    row_id = lax.broadcasted_iota(jnp.int32, (half - xrow, firm_dev), 0)
    for t in range(day_dev):
        lanes = slice(t * firm_dev, (t + 1) * firm_dev)
        big[xrow:half, lanes] = (row_id == d * day_dev + t).astype(f32).astype(jnp.bfloat16)
    if half > xrow:
        big[half + xrow:, :] = jnp.zeros((half - xrow, day_dev * firm_dev), jnp.bfloat16)
    load_mask.wait()
    mask = presence[...].astype(f32)
    for j in range(nd):
        masks[j] = mask[:, j * chunk:(j + 1) * chunk]
    here = presence[pl.ds(pl.multiple_of(d * day_dev, 8), day_dev), :].astype(f32)
    here_n = jnp.maximum(jnp.sum(here, axis=0, keepdims=True), 1.0)
    own = masks[d]
    counts = [
        jnp.sum(own[j * day_dev:(j + 1) * day_dev, :], axis=0, keepdims=True) for j in range(nd)
    ]
    n = functools.reduce(jnp.add, counts)
    day_id = lax.broadcasted_iota(jnp.int32, (days, chunk), 0)
    share = split(own / n)
    fill = jnp.zeros((xrow - crow, chunk), f32)
    tail = [jnp.zeros((half - xrow - days, chunk), f32)] if half > xrow + days else []

    pl.semaphore_wait(barrier, nf + nd - 2)
    sends = []
    alpha = []
    for q in tiles128:
        lanes = slice(q * 128, q * 128 + 128)
        load_panel[q].wait()
        total = on_day(q, 0, crow) * here[0:1, lanes]
        for t in range(1, day_dev):
            total = total + on_day(q, t, crow) * here[t:t + 1, lanes]
        alpha.append(total / here_n[:, lanes])
        for j in range(q * 128 // chunk, (q + 1) * 128 // chunk):
            first = j * chunk - q * 128
            alphas[j] = alpha[q][:, first:first + chunk]

            @pl.when(d != j)
            def _(j=j):
                pltpu.make_async_remote_copy(
                    src_ref=alphas.at[j], dst_ref=alphas_in.at[d], send_sem=s_a.at[j],
                    recv_sem=r_a.at[d], device_id=(f, j), device_id_type=MESH).start()

    alphas_in[d] = alphas[d]

    for q in tiles128:
        base = jnp.concatenate([alpha[q], jnp.zeros((xrow - crow, 128), f32)], axis=0)
        for t in range(day_dev):
            lanes = slice(t * firm_dev + q * 128, t * firm_dev + q * 128 + 128)
            hi, lo = split(here[t:t + 1, q * 128:q * 128 + 128] * (on_day(q, t, xrow) - base))
            big[:xrow, lanes] = hi
            big[half:half + xrow, lanes] = lo
    inner = nt16(jnp.concatenate([big[:xrow, :], big[half:half + xrow, :]], axis=0), big[...])

    for o in range(1, nd):
        src = day_peer(o)
        send_day(o, alphas.at[src], alphas_in.at[src], s_a, r_a.at[src]).wait_recv()
    blocks = [alphas_in[j] for j in range(nd)]
    mean = functools.reduce(jnp.add, [b * w for b, w in zip(blocks, counts)]) / n
    means_all[d] = mean
    for j in range(nd):
        lanes = slice(j * chunk, (j + 1) * chunk)
        delta = jnp.concatenate([blocks[j] - mean, fill], axis=0)
        first = j * day_dev
        dummy = jnp.where((day_id >= first) & (day_id < first + day_dev), own, 0.0)
        hi, lo = split(delta)
        left[:xrow, lanes] = hi
        left[xrow:2 * xrow, lanes] = lo
        left[2 * xrow:2 * xrow + days, lanes] = share[0]
        left[2 * xrow + days:, lanes] = share[1]
        hi, lo = split(jnp.concatenate([delta * counts[j], dummy] + tail, axis=0))
        right[:half, lanes] = hi
        right[half:, lanes] = lo
    outer = nt16(left[...], right[...])
    both = inner + outer[:2 * xrow, :]
    both = both[:, :half] + both[:, half:]
    table = jnp.concatenate(
        [both[:xrow, :] + both[xrow:, :],
         outer[2 * xrow:2 * xrow + days, :half] + outer[2 * xrow + days:, :half]], axis=0
    )

    if nf * piece > xrow + days:
        table = jnp.concatenate([table, jnp.zeros((nf * piece - xrow - days, width), f32)], axis=0)
    part[...] = table.reshape(nf, piece, width)
    for o in range(1, nf):
        c = send_firm(o, part.at[firm_peer(o)], part_in.at[f], s_1, r_1.at[f])
        c.start()
        sends.append(c)
    part_in[f] = part[f]
    for o in range(1, nf):
        src = firm_peer(o)
        send_firm(o, part.at[src], part_in.at[src], s_1, r_1.at[src]).wait_recv()
    mid[d] = functools.reduce(jnp.add, [part_in[j] for j in range(nf)])
    for o in range(1, nd):
        c = send_day(o, mid.at[d], mid.at[d], s_2, r_2.at[d])
        c.start()
        sends.append(c)
    for o in range(1, nd):
        c = send_day(o, means_all.at[d], means_all.at[d], s_m, r_m.at[d])
        c.start()
        sends.append(c)
    for o in range(1, nd):
        src = day_peer(o)
        send_day(o, mid.at[src], mid.at[src], s_2, r_2.at[src]).wait_recv()
    full[f] = functools.reduce(jnp.add, [mid[j] for j in range(nd)])
    for o in range(1, nf):
        c = send_firm(o, full.at[f], full.at[f], s_3, r_3.at[f])
        c.start()
        sends.append(c)
    for o in range(1, nf):
        src = firm_peer(o)
        send_firm(o, full.at[src], full.at[src], s_3, r_3.at[src]).wait_recv()

    table = full[...].reshape(nf * piece, width)
    csum = table[:xrow, xrow:xrow + days]
    cross = table[xrow:xrow + days, xrow:xrow + days]
    day_n = jnp.floor(jnp.sum(cross, axis=0, keepdims=True) + 0.5)
    before = csum / day_n
    after = before
    for _ in range(SWEEPS - 1):
        before, after = after, (csum + nn(after, cross)) / day_n
    step = after - before
    excess = step * day_n
    gram = table[:regs, :xrow] - (
        nt(csum[:regs], before) + nt(before[:regs], excess) + nt(excess[:regs], step)
    )

    tiles = eliminate(gram, regs)
    shape = (8, vfull.shape[1])
    sub = lax.broadcasted_iota(jnp.int32, shape, 0)
    lane = lax.broadcasted_iota(jnp.int32, shape, 1)
    picked = jnp.zeros(shape, f32)
    for i, t in enumerate(tiles):
        value = jnp.broadcast_to(t[:, regs:regs + 1], shape)
        vfull[8 * i:8 * i + 8, :] = -value
        picked = picked + jnp.where(lane == sub + 8 * i, value, 0.0)
    coef_ref[...] = jnp.sum(picked, axis=0, keepdims=True)[:, :regs]
    vfull[regs:, :] = jnp.where(
        lax.broadcasted_iota(jnp.int32, (xrow - regs, vfull.shape[1]), 0) == 0, 1.0, 0.0
    )

    acc = []
    for q in tiles128:
        terms = [panel[q, c * day_dev:(c + 1) * day_dev, :] * vfull[c:c + 1, :] for c in range(cols)]
        acc.append(functools.reduce(jnp.add, terms))
    acc = jnp.concatenate(acc, axis=1)
    v = vfull[:, :days]
    hi, lo = split(jnp.broadcast_to(jnp.sum(before * v, axis=0, keepdims=True), (8, days)))
    lead = jnp.concatenate([hi, lo], axis=0)
    spread = jnp.dot(lead, mask.astype(jnp.bfloat16), preferred_element_type=f32)
    spread = spread[0:1, :] + spread[8:9, :]
    day_part = jnp.sum(after * v, axis=0, keepdims=True)
    day_sel = (lax.broadcasted_iota(jnp.int32, (day_dev, days), 1)
               == lax.broadcasted_iota(jnp.int32, (day_dev, days), 0) + d * day_dev)
    day_here = jnp.sum(jnp.where(day_sel, day_part, 0.0), axis=1, keepdims=True)
    for o in range(1, nd):
        src = day_peer(o)
        send_day(o, means_all.at[src], means_all.at[src], s_m, r_m.at[src]).wait_recv()
    for j in range(nd):
        means[:, j * chunk:(j + 1) * chunk] = means_all[j]
    n_all = jnp.sum(mask, axis=0, keepdims=True)
    firm_part = jnp.concatenate(
        [jnp.sum(means[:, q:q + 128] * vfull[:crow, :], axis=0, keepdims=True)
         for q in range(0, firm_dev, 128)], axis=1) - spread / n_all
    resid_ref[...] = here * (acc - firm_part - day_here)

    for o in range(1, nd):
        to = day_peer(o)
        pltpu.make_async_remote_copy(
            src_ref=alphas.at[to], dst_ref=alphas_in.at[d], send_sem=s_a.at[to],
            recv_sem=r_a.at[d], device_id=(f, to), device_id_type=MESH).wait_send()
    for c in sends:
        c.wait_send()


def on_device(nf, nd, panel, presence, firm_count, day_count):
    cols, day_dev, firm_dev = panel.shape
    days = presence.shape[0]
    chunk = firm_dev // nd
    crow = up(cols, 8)
    xrow = up(cols, 16)
    half = up(xrow + days, 128)
    piece = up(-(-(xrow + days) // nf), 8)
    hbm = pl.BlockSpec(memory_space=pltpu.HBM)
    vm = pl.BlockSpec(memory_space=pltpu.VMEM)
    f32 = jnp.float32
    b16 = jnp.bfloat16
    dma = pltpu.SemaphoreType.DMA
    coef, resid = pl.pallas_call(
        functools.partial(kernel, nf, nd),
        out_shape=(jax.ShapeDtypeStruct((1, cols - 1), f32),
                   jax.ShapeDtypeStruct((day_dev, firm_dev), f32)),
        in_specs=[hbm, hbm],
        out_specs=(vm, vm),
        scratch_shapes=[
            pltpu.VMEM((firm_dev // 128, xrow * day_dev, 128), f32),
            pltpu.VMEM((days, firm_dev), jnp.int32),
            pltpu.VMEM((2 * half, day_dev * firm_dev), b16),
            pltpu.VMEM((2 * (xrow + days), firm_dev), b16),
            pltpu.VMEM((2 * half, firm_dev), b16),
            pltpu.VMEM((crow, firm_dev), f32),
            pltpu.VMEM((nd, crow, chunk), f32),
            pltpu.VMEM((nd, days, chunk), f32),
            pltpu.VMEM((nd, crow, chunk), f32),
            pltpu.VMEM((nd, crow, chunk), f32),
            pltpu.VMEM((nf, piece, half), f32),
            pltpu.VMEM((nf, piece, half), f32),
            pltpu.VMEM((nd, piece, half), f32),
            pltpu.VMEM((nf, piece, half), f32),
            pltpu.VMEM((xrow, 128), f32),
            dma((1 + firm_dev // 128,)), dma((nd,)), dma((nd,)), dma((nd,)), dma((nd,)),
            dma((nf,)), dma((nf,)), dma((nd,)), dma((nd,)), dma((nf,)), dma((nf,)),
        ],
        compiler_params=pltpu.CompilerParams(collective_id=0, has_side_effects=True),
    )(panel.reshape(cols * day_dev, firm_dev), presence)
    return coef.reshape(cols - 1), resid


def solution(mesh):
    placed = (P(None, "day", "firm"), P(None, "firm"), P("firm"), P())
    body = functools.partial(on_device, mesh.shape["firm"], mesh.shape["day"])
    return jax.shard_map(
        body, mesh=mesh, in_specs=placed, out_specs=(P(), P("day", "firm")), check_vma=False
    )
```

```python
import functools

import jax
import jax.numpy as jnp
from jax import lax
from jax.experimental import pallas as pl
from jax.experimental.pallas import tpu as pltpu
from jax.sharding import PartitionSpec as P

SWEEPS = 3
MESH = pl.DeviceIdType.MESH


def up(n, m):
    return -(-n // m) * m


def split(x):
    hi = x.astype(jnp.bfloat16)
    return hi, (x - hi.astype(jnp.float32)).astype(jnp.bfloat16)


def nt16(a, b):
    return lax.dot_general(a, b, (((1,), (1,)), ((), ())), preferred_element_type=jnp.float32)


def nt(a, b):
    a, b = split(a), split(b)
    return nt16(a[0], b[0]) + (nt16(a[0], b[1]) + nt16(a[1], b[0]))


def inverse2(p):
    (a, b), (c, e) = p
    det = a * e - b * c
    r = pl.reciprocal(det, approx=True)
    r = r * (2.0 - det * r)
    r = r * (2.0 - det * r)
    return [[e * r, -b * r], [-c * r, a * r]]


def times(p, rows):
    return [p[0][0] * rows[0] + p[0][1] * rows[1], p[1][0] * rows[0] + p[1][1] * rows[1]]


def solve4(p, rows):
    top = inverse2([p[0][:2], p[1][:2]])
    right = [[p[0][2], p[0][3]], [p[1][2], p[1][3]]]
    low = [p[2][:2], p[3][:2]]
    cols = [times(top, [right[0][j], right[1][j]]) for j in range(2)]
    schur = [[None, None], [None, None]]
    for j in range(2):
        down = times(low, cols[j])
        for i in range(2):
            schur[i][j] = p[2 + i][2 + j] - down[i]
    bottom = inverse2(schur)
    up_rows = times(top, rows[:2])
    down = times(low, up_rows)
    under = times(bottom, [rows[2] - down[0], rows[3] - down[1]])
    return [
        up_rows[0] - cols[0][0] * under[0] - cols[1][0] * under[1],
        up_rows[1] - cols[0][1] * under[0] - cols[1][1] * under[1],
    ] + under


def eliminate(mat, regs):
    tiles = [mat[8 * i:8 * i + 8, :] for i in range(regs // 8)]
    shape = tiles[0].shape
    sub = lax.broadcasted_iota(jnp.int32, shape, 0)
    for k in range(0, regs, 4):
        at, lo = k // 8, k % 8
        col = [[jnp.broadcast_to(t[:, k + j:k + j + 1], shape) for t in tiles] for j in range(4)]
        p = [[col[j][at][lo + i:lo + i + 1, :] for j in range(4)] for i in range(4)]
        rows = solve4(p, [tiles[at][lo + i:lo + i + 1, :] for i in range(4)])
        out = []
        for i, t in enumerate(tiles):
            t = t - (col[0][i] * rows[0] + col[1][i] * rows[1]) - (col[2][i] * rows[2] + col[3][i] * rows[3])
            if i == at:
                for j in range(4):
                    t = jnp.where(sub == lo + j, rows[j], t)
            out.append(t)
        tiles = out
    return tiles


def kernel(
    nf, nd, panel_hbm, presence_hbm, coef_ref, resid_ref,
    panel, presence, big, left, right, means, means_all, masks, alphas, alphas_in,
    part, part_in, mid, full, vfull,
    s_in, s_a, r_a, s_m, r_m, s_1, r_1, s_2, r_2, s_3, r_3,
):
    day_dev, firm_dev = resid_ref.shape
    cols = panel_hbm.shape[0] // day_dev
    regs = cols - 1
    days = presence.shape[0]
    chunk = firm_dev // nd
    crow = up(cols, 8)
    xrow = panel.shape[1] // day_dev
    tiles128 = range(firm_dev // 128)
    half = right.shape[0] // 2
    piece, width = part.shape[1:]
    f = lax.axis_index("firm")
    d = lax.axis_index("day")
    f32 = jnp.float32

    def firm_peer(o):
        return lax.rem(f + o, nf)

    def day_peer(o):
        return lax.rem(d + o, nd)

    load_mask = pltpu.make_async_copy(presence_hbm, presence, s_in.at[0])
    load_mask.start()
    load_panel = [
        pltpu.make_async_copy(
            panel_hbm.at[:, pl.ds(q * 128, 128)], panel.at[q, pl.ds(0, cols * day_dev)], s_in.at[1 + q])
        for q in tiles128
    ]
    for c in load_panel:
        c.start()
    barrier = pltpu.get_barrier_semaphore()
    for o in range(1, nf):
        pl.semaphore_signal(barrier, inc=1, device_id=(firm_peer(o), d), device_id_type=MESH)
    for o in range(1, nd):
        pl.semaphore_signal(barrier, inc=1, device_id=(f, day_peer(o)), device_id_type=MESH)

    def send_day(o, src, dst, ssem, rsem):
        return pltpu.make_async_remote_copy(
            src_ref=src, dst_ref=dst, send_sem=ssem.at[o], recv_sem=rsem,
            device_id=(f, day_peer(o)), device_id_type=MESH)

    def send_firm(o, src, dst, ssem, rsem):
        return pltpu.make_async_remote_copy(
            src_ref=src, dst_ref=dst, send_sem=ssem.at[o], recv_sem=rsem,
            device_id=(firm_peer(o), d), device_id_type=MESH)

    panel[:, cols * day_dev:, :] = jnp.zeros((len(tiles128), (xrow - cols) * day_dev, 128), f32)

    def on_day(q, t, rows):
        return panel[q, pl.ds(t, rows, stride=day_dev), :]

    row_id = lax.broadcasted_iota(jnp.int32, (half - xrow, firm_dev), 0)
    for t in range(day_dev):
        lanes = slice(t * firm_dev, (t + 1) * firm_dev)
        big[xrow:half, lanes] = (row_id == d * day_dev + t).astype(f32).astype(jnp.bfloat16)
    if half > xrow:
        big[half + xrow:, :] = jnp.zeros((half - xrow, day_dev * firm_dev), jnp.bfloat16)
    load_mask.wait()
    mask = presence[...].astype(f32)
    for j in range(nd):
        masks[j] = mask[:, j * chunk:(j + 1) * chunk]
    here = presence[pl.ds(pl.multiple_of(d * day_dev, 8), day_dev), :].astype(f32)
    here_n = jnp.maximum(jnp.sum(here, axis=0, keepdims=True), 1.0)
    own = masks[d]
    counts = [
        jnp.sum(own[j * day_dev:(j + 1) * day_dev, :], axis=0, keepdims=True) for j in range(nd)
    ]
    n = functools.reduce(jnp.add, counts)
    day_id = lax.broadcasted_iota(jnp.int32, (days, chunk), 0)
    share = split(own / n)
    fill = jnp.zeros((xrow - crow, chunk), f32)
    tail = [jnp.zeros((half - xrow - days, chunk), f32)] if half > xrow + days else []

    pl.semaphore_wait(barrier, nf + nd - 2)
    sends = []
    alpha = []
    for q in tiles128:
        lanes = slice(q * 128, q * 128 + 128)
        load_panel[q].wait()
        total = on_day(q, 0, crow) * here[0:1, lanes]
        for t in range(1, day_dev):
            total = total + on_day(q, t, crow) * here[t:t + 1, lanes]
        alpha.append(total / here_n[:, lanes])
        for j in range(q * 128 // chunk, (q + 1) * 128 // chunk):
            first = j * chunk - q * 128
            alphas[j] = alpha[q][:, first:first + chunk]

            @pl.when(d != j)
            def _(j=j):
                pltpu.make_async_remote_copy(
                    src_ref=alphas.at[j], dst_ref=alphas_in.at[d], send_sem=s_a.at[j],
                    recv_sem=r_a.at[d], device_id=(f, j), device_id_type=MESH).start()

    alphas_in[d] = alphas[d]

    for q in tiles128:
        base = jnp.concatenate([alpha[q], jnp.zeros((xrow - crow, 128), f32)], axis=0)
        for t in range(day_dev):
            lanes = slice(t * firm_dev + q * 128, t * firm_dev + q * 128 + 128)
            hi, lo = split(here[t:t + 1, q * 128:q * 128 + 128] * (on_day(q, t, xrow) - base))
            big[:xrow, lanes] = hi
            big[half:half + xrow, lanes] = lo
    inner = nt16(jnp.concatenate([big[:xrow, :], big[half:half + xrow, :]], axis=0), big[...])

    for o in range(1, nd):
        src = day_peer(o)
        send_day(o, alphas.at[src], alphas_in.at[src], s_a, r_a.at[src]).wait_recv()
    blocks = [alphas_in[j] for j in range(nd)]
    mean = functools.reduce(jnp.add, [b * w for b, w in zip(blocks, counts)]) / n
    means_all[d] = mean
    for j in range(nd):
        lanes = slice(j * chunk, (j + 1) * chunk)
        delta = jnp.concatenate([blocks[j] - mean, fill], axis=0)
        first = j * day_dev
        dummy = jnp.where((day_id >= first) & (day_id < first + day_dev), own, 0.0)
        hi, lo = split(delta)
        left[:xrow, lanes] = hi
        left[xrow:2 * xrow, lanes] = lo
        left[2 * xrow:2 * xrow + days, lanes] = share[0]
        left[2 * xrow + days:, lanes] = share[1]
        hi, lo = split(jnp.concatenate([delta * counts[j], dummy] + tail, axis=0))
        right[:half, lanes] = hi
        right[half:, lanes] = lo
    outer = nt16(left[...], right[...])
    both = inner + outer[:2 * xrow, :]
    both = both[:, :half] + both[:, half:]
    table = jnp.concatenate(
        [both[:xrow, :] + both[xrow:, :],
         outer[2 * xrow:2 * xrow + days, :half] + outer[2 * xrow + days:, :half]], axis=0
    )

    if nf * piece > xrow + days:
        table = jnp.concatenate([table, jnp.zeros((nf * piece - xrow - days, width), f32)], axis=0)
    part[...] = table.reshape(nf, piece, width)
    for o in range(1, nf):
        c = send_firm(o, part.at[firm_peer(o)], part_in.at[f], s_1, r_1.at[f])
        c.start()
        sends.append(c)
    part_in[f] = part[f]
    for o in range(1, nf):
        src = firm_peer(o)
        send_firm(o, part.at[src], part_in.at[src], s_1, r_1.at[src]).wait_recv()
    mid[d] = functools.reduce(jnp.add, [part_in[j] for j in range(nf)])
    for o in range(1, nd):
        c = send_day(o, mid.at[d], mid.at[d], s_2, r_2.at[d])
        c.start()
        sends.append(c)
    for o in range(1, nd):
        c = send_day(o, means_all.at[d], means_all.at[d], s_m, r_m.at[d])
        c.start()
        sends.append(c)
    for o in range(1, nd):
        src = day_peer(o)
        send_day(o, mid.at[src], mid.at[src], s_2, r_2.at[src]).wait_recv()
    full[f] = functools.reduce(jnp.add, [mid[j] for j in range(nd)])
    for o in range(1, nf):
        c = send_firm(o, full.at[f], full.at[f], s_3, r_3.at[f])
        c.start()
        sends.append(c)
    for o in range(1, nf):
        src = firm_peer(o)
        send_firm(o, full.at[src], full.at[src], s_3, r_3.at[src]).wait_recv()

    table = full[...].reshape(nf * piece, width)
    csum = table[:xrow, xrow:xrow + days]
    cross = table[xrow:xrow + days, xrow:xrow + days]
    day_n = jnp.floor(jnp.sum(cross, axis=0, keepdims=True) + 0.5)
    before = csum / day_n
    after = before
    for _ in range(SWEEPS - 1):
        before, after = after, (csum + nt(after, cross)) / day_n
    step = after - before
    excess = step * day_n
    gram = table[:regs, :xrow] - (
        nt(csum[:regs], before) + nt(before[:regs], excess) + nt(excess[:regs], step)
    )

    tiles = eliminate(gram, regs)
    shape = (8, vfull.shape[1])
    sub = lax.broadcasted_iota(jnp.int32, shape, 0)
    lane = lax.broadcasted_iota(jnp.int32, shape, 1)
    picked = jnp.zeros(shape, f32)
    for i, t in enumerate(tiles):
        value = jnp.broadcast_to(t[:, regs:regs + 1], shape)
        vfull[8 * i:8 * i + 8, :] = -value
        picked = picked + jnp.where(lane == sub + 8 * i, value, 0.0)
    coef_ref[...] = jnp.sum(picked, axis=0, keepdims=True)[:, :regs]
    vfull[regs:, :] = jnp.where(
        lax.broadcasted_iota(jnp.int32, (xrow - regs, vfull.shape[1]), 0) == 0, 1.0, 0.0
    )

    acc = []
    for q in tiles128:
        terms = [panel[q, c * day_dev:(c + 1) * day_dev, :] * vfull[c:c + 1, :] for c in range(cols)]
        acc.append(functools.reduce(jnp.add, terms))
    acc = jnp.concatenate(acc, axis=1)
    v = vfull[:, :days]
    hi, lo = split(jnp.broadcast_to(jnp.sum(before * v, axis=0, keepdims=True), (8, days)))
    lead = jnp.concatenate([hi, lo], axis=0)
    spread = jnp.dot(lead, mask.astype(jnp.bfloat16), preferred_element_type=f32)
    spread = spread[0:1, :] + spread[8:9, :]
    day_part = jnp.sum(after * v, axis=0, keepdims=True)
    day_sel = (lax.broadcasted_iota(jnp.int32, (day_dev, days), 1)
               == lax.broadcasted_iota(jnp.int32, (day_dev, days), 0) + d * day_dev)
    day_here = jnp.sum(jnp.where(day_sel, day_part, 0.0), axis=1, keepdims=True)
    for o in range(1, nd):
        src = day_peer(o)
        send_day(o, means_all.at[src], means_all.at[src], s_m, r_m.at[src]).wait_recv()
    for j in range(nd):
        means[:, j * chunk:(j + 1) * chunk] = means_all[j]
    n_all = jnp.sum(mask, axis=0, keepdims=True)
    firm_part = jnp.concatenate(
        [jnp.sum(means[:, q:q + 128] * vfull[:crow, :], axis=0, keepdims=True)
         for q in range(0, firm_dev, 128)], axis=1) - spread / n_all
    resid_ref[...] = here * (acc - firm_part - day_here)

    for o in range(1, nd):
        to = day_peer(o)
        pltpu.make_async_remote_copy(
            src_ref=alphas.at[to], dst_ref=alphas_in.at[d], send_sem=s_a.at[to],
            recv_sem=r_a.at[d], device_id=(f, to), device_id_type=MESH).wait_send()
    for c in sends:
        c.wait_send()


def on_device(nf, nd, panel, presence, firm_count, day_count):
    cols, day_dev, firm_dev = panel.shape
    days = presence.shape[0]
    chunk = firm_dev // nd
    crow = up(cols, 8)
    xrow = up(cols, 16)
    half = up(xrow + days, 128)
    piece = up(-(-(xrow + days) // nf), 8)
    hbm = pl.BlockSpec(memory_space=pltpu.HBM)
    vm = pl.BlockSpec(memory_space=pltpu.VMEM)
    f32 = jnp.float32
    b16 = jnp.bfloat16
    dma = pltpu.SemaphoreType.DMA
    coef, resid = pl.pallas_call(
        functools.partial(kernel, nf, nd),
        out_shape=(jax.ShapeDtypeStruct((1, cols - 1), f32),
                   jax.ShapeDtypeStruct((day_dev, firm_dev), f32)),
        in_specs=[hbm, hbm],
        out_specs=(vm, vm),
        scratch_shapes=[
            pltpu.VMEM((firm_dev // 128, xrow * day_dev, 128), f32),
            pltpu.VMEM((days, firm_dev), jnp.int32),
            pltpu.VMEM((2 * half, day_dev * firm_dev), b16),
            pltpu.VMEM((2 * (xrow + days), firm_dev), b16),
            pltpu.VMEM((2 * half, firm_dev), b16),
            pltpu.VMEM((crow, firm_dev), f32),
            pltpu.VMEM((nd, crow, chunk), f32),
            pltpu.VMEM((nd, days, chunk), f32),
            pltpu.VMEM((nd, crow, chunk), f32),
            pltpu.VMEM((nd, crow, chunk), f32),
            pltpu.VMEM((nf, piece, half), f32),
            pltpu.VMEM((nf, piece, half), f32),
            pltpu.VMEM((nd, piece, half), f32),
            pltpu.VMEM((nf, piece, half), f32),
            pltpu.VMEM((xrow, 128), f32),
            dma((1 + firm_dev // 128,)), dma((nd,)), dma((nd,)), dma((nd,)), dma((nd,)),
            dma((nf,)), dma((nf,)), dma((nd,)), dma((nd,)), dma((nf,)), dma((nf,)),
        ],
        compiler_params=pltpu.CompilerParams(collective_id=0, has_side_effects=True),
    )(panel.reshape(cols * day_dev, firm_dev), presence)
    return coef.reshape(cols - 1), resid


def solution(mesh):
    placed = (P(None, "day", "firm"), P(None, "firm"), P("firm"), P())
    body = functools.partial(on_device, mesh.shape["firm"], mesh.shape["day"])
    return jax.shard_map(
        body, mesh=mesh, in_specs=placed, out_specs=(P(), P("day", "firm")), check_vma=False
    )
```
